512 devices in a mesh: row: 16 (over z, core), col: 32 (over x, y).
Axes of the slice: x: 4, y: 8, z: 8, core: 2. Of those that a mesh axis runs over, the one named last changes fastest.
Arguments:
- tensor3: bfloat16 [512, 2048, 512], P('row', 'col'), may hold values from -6 to 6
- pair_mask: int32 [8, 32], P(None, 'col'), may hold values 0 or 1
- g_occ: bfloat16 [512, 512], replicated, may hold values from -0.25 to 0.25
- g_virt_band: bfloat16 [2048, 192], P('col'), may hold values from -0.4375 to 0.4375
Outputs:
- chi: float32 [512, 512], P('row', 'col')
The draws below stay inside these ranges and needn't reach their ends.
All inputs are finite; a program needn't handle non-finite values. No bound on the sum of `pair_mask` on one device may be relied on, other than what follows from the above.
Results may differ from the reference program's by a relative error of at most 0.0041.
Values may be sent and summed in bfloat16 or wider, within the bound.
A program may use at most 64 MiB of HBM per device.

```python
import math
import jax
import jax.numpy as jnp
from jax import lax

BS = 64
NBM = 8
NM = 512
NLB = 32
NL = 2048
NAUX = 512


def touch_ends(values, rng, smallest, largest):
    longest = values.shape.index(max(values.shape))
    spots = []
    for shift in (0, 1):
        where = [jax.random.randint(jax.random.fold_in(rng, axis), (), 0, length) for axis, length in enumerate(values.shape)]
        where[longest] = (where[longest] + shift) % values.shape[longest]
        spots.append(tuple(where))
    return values.at[spots[0]].set(smallest).at[spots[1]].set(largest)


def block_scale(own_key, dims, shards, least, top_value):
    level, own = 1.0, jax.random.fold_in(own_key, 6)
    for dim, shards_of in shards:
        heights = jnp.exp(jax.random.uniform(jax.random.fold_in(own, dim), (shards_of,), jnp.float32, least / len(shards), top_value / len(shards)))
        level = level * jnp.repeat(heights, dims[dim] // shards_of).reshape([-1 if axis == dim else 1 for axis in range(len(dims))])
    return level


def scatter_about(own_key, dims, width, bound, pieces=(), kind=jnp.bfloat16):
    entries = jax.random.normal(own_key, dims, jnp.float32) * width
    if len(pieces) > 0:
        entries = block_scale(own_key, dims, pieces, -0.22, 0.18) * entries
    return jnp.clip(entries, min=-bound, max=bound).astype(kind)


def setup_inputs(seed: int = 0) -> dict:
    arg_keys = jax.random.split(jax.random.key(seed), 5)
    tensor3 = scatter_about(arg_keys[0], (NAUX, NL, NM), 1.0, 6.0, ((0, 16), (1, 32)))
    pair_mask = touch_ends((jax.random.randint(arg_keys[1], (NBM, NLB), 0, 3) < 2).astype(jnp.int32), jax.random.fold_in(arg_keys[1], 1), 0, 1)
    g_occ = scatter_about(arg_keys[2], (NM, NM), NM ** -0.5, 0.25)
    g_virt_band = scatter_about(arg_keys[3], (NL, 3 * BS), (3 * BS) ** -0.5, 0.4375, ((0, 32),))
    return {"tensor3": tensor3, "pair_mask": pair_mask, "g_occ": g_occ, "g_virt_band": g_virt_band}


def block_slab(tensor3, pair_mask, index):
    inside = jnp.logical_and(index >= 0, index < NLB)
    safe = jnp.clip(index, 0, NLB - 1).astype(jnp.int32)
    slab = lax.dynamic_slice_in_dim(tensor3, safe * BS, BS, 1)
    column = lax.dynamic_slice_in_dim(pair_mask, safe, 1, 1)[:, 0]
    keep = jnp.repeat(column, BS) * inside.astype(jnp.int32)
    return jnp.where(keep[None, None, :] > 0, slab, jnp.zeros_like(slab))

def reference(tensor3, pair_mask, g_occ, g_virt_band):
    factor = 1.0 / math.sqrt(NM * NL)
    occ_matrix = g_occ.astype(jnp.float32)

    def advance(total, index):
        current = block_slab(tensor3, pair_mask, index)
        window = jnp.concatenate([block_slab(tensor3, pair_mask, index - 1), current, block_slab(tensor3, pair_mask, index + 1)], axis=1)
        occ_part = jnp.einsum('plm,mn->pln', current.astype(jnp.float32), occ_matrix).astype(jnp.bfloat16)
        band = lax.dynamic_slice_in_dim(g_virt_band, (index * BS).astype(jnp.int32), BS, 0)
        virt_part = jnp.einsum('qsn,ls->qln', window.astype(jnp.float32), band.astype(jnp.float32)).astype(jnp.bfloat16)
        total = total + jnp.einsum('pln,qln->pq', occ_part.astype(jnp.float32), virt_part.astype(jnp.float32))
        return (total, None)
    total, unused = lax.scan(advance, jnp.zeros((NAUX, NAUX), jnp.float32), jnp.arange(NLB, dtype=jnp.int32))
    return total * factor
```

```python
import math

import jax
import jax.numpy as jnp
from jax import lax
from jax.experimental import pallas as pl
from jax.experimental.pallas import tpu as pltpu
from jax.sharding import PartitionSpec as P

MESH = pl.DeviceIdType.MESH
ROWS, NX, NY = 16, 4, 8
COLS = NX * NY
BS, AUX, ORB = 64, 32, 512
LANES, PIECE = 128, 16
F32, BF16 = jnp.float32, jnp.bfloat16


def remote(src, dst, send, recv, where):
    return pltpu.make_async_remote_copy(
        src_ref=src, dst_ref=dst, send_sem=send, recv_sem=recv, device_id=where, device_id_type=MESH
    )


def kernel(
    m_ref, pm_ref, g_ref, gv_ref, out_ref,
    mk, halo, a_send, b_send, a_in, b_in, acc, xs, xr, ys, yr, zs, zr, tr,
    h_ss, h_rs, a_ss, a_rs, b_ss, b_rs, x_ss, x_rs, y_ss, y_rs, z_ss, z_rs,
):
    r = lax.axis_index("row")
    c = lax.axis_index("col")
    x, y = c // NY, c % NY
    lg_me, ng_me = r // 4, r % 4

    barrier = pltpu.get_barrier_semaphore()

    def greet(where):
        pl.semaphore_signal(barrier, inc=1, device_id=where, device_id_type=MESH)

    @pl.loop(1, ROWS)
    def _(k):
        greet({"row": (r + k) % ROWS})

    for k in range(1, NX):
        greet({"col": ((x + k) % NX) * NY + y})

    @pl.loop(1, NY)
    def _(k):
        greet({"col": x * NY + (y + k) % NY})

    @pl.when(c > 0)
    def _():
        greet({"col": c - 1})

    @pl.when(c < COLS - 1)
    def _():
        greet({"col": c + 1})

    kept = (pm_ref[...] > 0).astype(F32)
    lane = lax.broadcasted_iota(jnp.int32, (8, ORB), 1) // BS
    rows8 = lax.broadcasted_iota(jnp.int32, (8, ORB), 0)
    keep = jnp.sum(jnp.where(lane == rows8, jnp.broadcast_to(kept, (8, ORB)), 0.0), axis=0, keepdims=True)

    both = (c > 0).astype(jnp.int32) + (c < COLS - 1).astype(jnp.int32)
    pl.semaphore_wait(barrier, ROWS - 1 + NX - 1 + NY - 1 + both)

    def to_right(ng):
        return remote(mk.at[ng], halo.at[0, ng], h_ss.at[0, ng], h_rs.at[0, ng], {"col": c + 1})

    def to_left(ng):
        return remote(mk.at[ng], halo.at[1, ng], h_ss.at[1, ng], h_rs.at[1, ng], {"col": c - 1})

    for ng in range(4):
        k_ng = keep[:, ng * LANES:(ng + 1) * LANES].astype(BF16).reshape(1, LANES)

        @pl.loop(0, AUX)
        def _(p):
            mk[ng, p] = m_ref[p, :, ng * LANES:(ng + 1) * LANES] * k_ng

        @pl.when(c < COLS - 1)
        def _():
            to_right(ng).start()

        @pl.when(c > 0)
        def _():
            to_left(ng).start()

    @pl.when(c == 0)
    def _():
        halo[0] = jnp.zeros((4, AUX, BS, LANES), BF16)

    @pl.when(c == COLS - 1)
    def _():
        halo[1] = jnp.zeros((4, AUX, BS, LANES), BF16)

    @pl.loop(0, 4)
    def _(lg):
        for ph in range(2):
            rows = [
                mk[ng, ph * 16:(ph + 1) * 16, pl.ds(pl.multiple_of(lg * 16, 16), 16), :].reshape(256, LANES)
                for ng in range(4)
            ]
            left = jnp.concatenate(rows, axis=1)
            for nh in range(2):
                part = jnp.dot(left, g_ref[:, nh * 256:(nh + 1) * 256], preferred_element_type=F32)
                for ns in range(2):
                    piece = part[:, ns * LANES:(ns + 1) * LANES].reshape(16, 16, LANES)
                    piece = jnp.transpose(piece, (1, 0, 2)).astype(BF16)
                    a_send[nh * 2 + ns, pl.ds(lg * 16, 16), ph * 16:(ph + 1) * 16, :] = piece

    def send_a(d):
        return remote(
            a_send.at[d % 4, pl.ds((d // 4) * 16, 16)], a_in.at[r], a_ss.at[d], a_rs.at[r], {"row": d}
        )

    def send_b(d):
        return remote(
            b_send.at[d % 4, pl.ds((d // 4) * 16, 16)], b_in.at[r], b_ss.at[d], b_rs.at[r], {"row": d}
        )

    @pl.loop(0, ROWS - 1)
    def _(i):
        half = i // 2 + 1
        step = half + (i % 2) * (ROWS - 2 * half)
        send_a((r + step) % ROWS).start()

    a_in[r] = a_send[ng_me, pl.ds(lg_me * 16, 16)]

    band = gv_ref[...]
    for ng in range(4):
        @pl.when(c > 0)
        def _():
            to_right(ng).wait_recv()

        @pl.when(c < COLS - 1)
        def _():
            to_left(ng).wait_recv()

        @pl.loop(0, 2)
        def _(qh):
            outs = []
            for qp in range(8):
                wide = []
                for q in range(2):
                    at = qh * 16 + qp * 2 + q
                    wide.append(jnp.concatenate([halo[0, ng, at], mk[ng, at], halo[1, ng, at]], axis=0))
                prod = jnp.dot(band, jnp.concatenate(wide, axis=1), preferred_element_type=F32)
                outs += [prod[:, :LANES], prod[:, LANES:]]
            full = jnp.transpose(jnp.stack(outs, axis=0), (1, 0, 2)).astype(BF16)
            b_send[ng, :, pl.ds(pl.multiple_of(qh * 16, 16), 16), :] = full

        @pl.loop(0, 4)
        def _(j):
            d = ((lg_me + j) % 4) * 4 + ng

            @pl.when(d != r)
            def _():
                send_b(d).start()

    b_in[r] = b_send[ng_me, pl.ds(lg_me * 16, 16)]

    @pl.loop(1, ROWS)
    def _(k):
        s = (r + k) % ROWS
        remote(a_send.at[0, pl.ds(0, 16)], a_in.at[s], a_ss.at[s], a_rs.at[s], {"row": s}).wait_recv()

    acc[...] = jnp.zeros_like(acc)

    @pl.loop(1, ROWS)
    def _(k):
        s = (r + k) % ROWS
        remote(b_send.at[0, pl.ds(0, 16)], b_in.at[s], b_ss.at[s], b_rs.at[s], {"row": s}).wait_recv()

    @pl.loop(0, 8)
    def _(l):
        def pair(ref):
            return jnp.concatenate(
                [ref[:, 2 * l].reshape(512, LANES), ref[:, 2 * l + 1].reshape(512, LANES)], axis=1
            )
        acc[...] += lax.dot_general(
            pair(b_in), pair(a_in), (((1,), (1,)), ((), ())), preferred_element_type=F32
        )

    for i in range(NX):
        xs[i] = acc[i * 128:(i + 1) * 128, :].astype(BF16)

    def send_x(k):
        to = (x + k) % NX
        return remote(xs.at[to], xr.at[k], x_ss.at[k], x_rs.at[k], {"col": to * NY + y})

    for k in range(1, NX):
        send_x(k).start()
    for k in range(1, NX):
        send_x(k).wait_recv()
    mine = acc[pl.ds(pl.multiple_of(x * 128, 128), 128), :]
    for k in range(1, NX):
        mine = mine + xr[k].astype(F32)

    for i in range(NY):
        ys[i] = mine[i * 16:(i + 1) * 16, :].astype(BF16)
    acc[0:128, :] = mine

    def send_y(k):
        to = (y + k) % NY
        return remote(ys.at[to], yr.at[k], y_ss.at[k], y_rs.at[k], {"col": x * NY + to})

    for k in range(1, NY):
        send_y(k).start()
    for k in range(1, NY):
        send_y(k).wait_recv()
    own = acc[pl.ds(pl.multiple_of(y * 16, 16), 16), :]
    for k in range(1, NY):
        own = own + yr[k].astype(F32)
    for i in range(4):
        zs[i] = own[:, i * LANES:(i + 1) * LANES]

    def send_z(k):
        to = (r + k) % ROWS
        return remote(zs.at[to // 4], zr.at[k], z_ss.at[k], z_rs.at[k], {"row": to})

    @pl.loop(1, ROWS)
    def _(k):
        send_z(k).start()

    zr[0] = zs[lg_me]

    @pl.loop(1, ROWS)
    def _(k):
        send_z(k).wait_recv()

    total = jnp.sum(zr[...], axis=0)
    tr[...] = jnp.transpose(total, (1, 0))
    factor = 1.0 / math.sqrt(ORB * BS * COLS)
    out_ref[...] = tr[pl.ds(pl.multiple_of(ng_me * AUX, AUX), AUX), :] * factor

    for ng in range(4):
        @pl.when(c < COLS - 1)
        def _():
            to_right(ng).wait_send()

        @pl.when(c > 0)
        def _():
            to_left(ng).wait_send()

    @pl.loop(1, ROWS)
    def _(k):
        d = (r + k) % ROWS
        send_a(d).wait_send()
        send_b(d).wait_send()
        send_z(k).wait_send()

    for k in range(1, NX):
        send_x(k).wait_send()
    for k in range(1, NY):
        send_y(k).wait_send()


def on_device(tensor3, pair_mask, g_occ, g_virt_band):
    vmem = pl.BlockSpec(memory_space=pltpu.VMEM)
    dma = pltpu.SemaphoreType.DMA
    return pl.pallas_call(
        kernel,
        out_shape=jax.ShapeDtypeStruct((AUX, 16), F32),
        in_specs=[vmem] * 4,
        out_specs=vmem,
        scratch_shapes=[
            pltpu.VMEM((4, AUX, BS, LANES), BF16),
            pltpu.VMEM((2, 4, AUX, BS, LANES), BF16),
            pltpu.VMEM((4, BS, AUX, LANES), BF16),
            pltpu.VMEM((4, BS, AUX, LANES), BF16),
            pltpu.VMEM((ROWS, PIECE, AUX, LANES), BF16),
            pltpu.VMEM((ROWS, PIECE, AUX, LANES), BF16),
            pltpu.VMEM((512, 512), F32),
            pltpu.VMEM((NX, 128, 512), BF16),
            pltpu.VMEM((NX, 128, 512), BF16),
            pltpu.VMEM((NY, 16, 512), BF16),
            pltpu.VMEM((NY, 16, 512), BF16),
            pltpu.VMEM((4, 16, LANES), F32),
            pltpu.VMEM((ROWS, 16, LANES), F32),
            pltpu.VMEM((LANES, 16), F32),
            dma((2, 4)), dma((2, 4)),
            dma((ROWS,)), dma((ROWS,)), dma((ROWS,)), dma((ROWS,)),
            dma((NX,)), dma((NX,)), dma((NY,)), dma((NY,)), dma((ROWS,)), dma((ROWS,)),
        ],
        compiler_params=pltpu.CompilerParams(
            collective_id=0, has_side_effects=True, vmem_limit_bytes=48 * 1024 * 1024
        ),
        cost_estimate=pl.CostEstimate(flops=2600000000, bytes_accessed=3 << 20, transcendentals=0),
    )(tensor3, pair_mask, g_occ, g_virt_band)


def solution(mesh):
    return jax.shard_map(
        on_device,
        mesh=mesh,
        in_specs=(P("row", "col", None), P(None, "col"), P(), P("col", None)),
        out_specs=P("row", "col"),
        check_vma=False,
    )
```

```python
import math

import jax
import jax.numpy as jnp
from jax import lax
from jax.experimental import pallas as pl
from jax.experimental.pallas import tpu as pltpu
from jax.sharding import PartitionSpec as P

MESH = pl.DeviceIdType.MESH
ROWS, NX, NY = 16, 4, 8
COLS = NX * NY
BS, AUX, ORB = 64, 32, 512
LANES, PIECE, HALF = 128, 16, 16
F32, BF16 = jnp.float32, jnp.bfloat16


def remote(src, dst, send, recv, where):
    return pltpu.make_async_remote_copy(
        src_ref=src, dst_ref=dst, send_sem=send, recv_sem=recv, device_id=where, device_id_type=MESH
    )


def kernel(
    m_hbm, pm_hbm, g_hbm, gv_hbm, out_ref,
    m_ref, pm_ref, g_ref, gv_ref, mk, halo, a_send, b_send, a_in, b_in,
    acc, part, xs, xr, ys, yr, zs, zr, tr,
    in_s, h_ss, h_rs, a_ss, a_rs, b_ss, b_rs, x_ss, x_rs, y_ss, y_rs, z_ss, z_rs,
):
    r = lax.axis_index("row")
    c = lax.axis_index("col")
    x, y = c // NY, c % NY
    lg_me, ng_me = r // 4, r % 4

    def load_m(i):
        return pltpu.make_async_copy(m_hbm.at[pl.ds(8 * i, 8)], m_ref.at[pl.ds(8 * i, 8)], in_s.at[i])

    load_pm = pltpu.make_async_copy(pm_hbm, pm_ref, in_s.at[4])
    load_g = pltpu.make_async_copy(g_hbm, g_ref, in_s.at[5])
    load_gv = pltpu.make_async_copy(gv_hbm, gv_ref, in_s.at[6])
    load_pm.start()
    for i in range(4):
        load_m(i).start()
    load_g.start()
    load_gv.start()

    barrier = pltpu.get_barrier_semaphore()

    def greet(where):
        pl.semaphore_signal(barrier, inc=1, device_id=where, device_id_type=MESH)

    @pl.loop(1, ROWS)
    def _(k):
        greet({"row": (r + k) % ROWS})

    for k in range(1, NX):
        greet({"col": ((x + k) % NX) * NY + y})

    @pl.loop(1, NY)
    def _(k):
        greet({"col": x * NY + (y + k) % NY})

    @pl.when(c > 0)
    def _():
        greet({"col": c - 1})

    @pl.when(c < COLS - 1)
    def _():
        greet({"col": c + 1})

    load_pm.wait()
    lane = lax.broadcasted_iota(jnp.int32, (1, ORB), 1) // BS
    keep = jnp.zeros((1, ORB), F32)
    for b in range(8):
        kept = jnp.broadcast_to((pm_ref[0:1, b:b + 1] > 0).astype(F32), (1, ORB))
        keep = jnp.where(lane == b, kept, keep)
    keep = keep.astype(BF16)

    for i in range(4):
        load_m(i).wait()

        @pl.loop(8 * i, 8 * i + 8)
        def _(p):
            row = m_ref[p] * keep
            for ng in range(4):
                mk[ng, p] = row[:, ng * LANES:(ng + 1) * LANES]

    def occ(lg):
        for ph in range(2):
            rows = [
                mk[ng, ph * 16:(ph + 1) * 16, pl.ds(pl.multiple_of(lg * 16, 16), 16), :].reshape(256, LANES)
                for ng in range(4)
            ]
            left = jnp.concatenate(rows, axis=1)
            for nh in range(2):
                part = jnp.dot(left, g_ref[:, nh * 256:(nh + 1) * 256], preferred_element_type=F32)
                for ns in range(2):
                    piece = part[:, ns * LANES:(ns + 1) * LANES].reshape(16, 16, LANES)
                    piece = jnp.transpose(piece, (1, 0, 2)).astype(BF16)
                    a_send[nh * 2 + ns, pl.ds(lg * 16, 16), ph * 16:(ph + 1) * 16, :] = piece

    def send_a(d):
        return remote(
            a_send.at[d % 4, pl.ds((d // 4) * 16, 16)], a_in.at[r], a_ss.at[d], a_rs.at[r], {"row": d}
        )

    load_g.wait()

    @pl.loop(0, 4)
    def _(lg):
        occ(lg)

    both = (c > 0).astype(jnp.int32) + (c < COLS - 1).astype(jnp.int32)
    pl.semaphore_wait(barrier, ROWS - 1 + NX - 1 + NY - 1 + both)

    def half_of(ref, g):
        return ref.at[:, pl.ds(HALF * g, HALF)]

    def to_right(g):
        return remote(half_of(mk, g), half_of(halo.at[0], g), h_ss.at[0, g], h_rs.at[0, g], {"col": c + 1})

    def to_left(g):
        return remote(half_of(mk, g), half_of(halo.at[1], g), h_ss.at[1, g], h_rs.at[1, g], {"col": c - 1})

    def ordered(i):
        near = i // 2 + 1
        return (r + near + (i % 2) * (ROWS - 2 * near)) % ROWS

    @pl.loop(0, 4)
    def _(i):
        send_a(ordered(i)).start()

    for g in range(2):
        @pl.when(c < COLS - 1)
        def _():
            to_right(g).start()

        @pl.when(c > 0)
        def _():
            to_left(g).start()

    @pl.loop(4, ROWS - 1)
    def _(i):
        send_a(ordered(i)).start()

    a_in[r] = a_send[ng_me, pl.ds(lg_me * 16, 16)]

    @pl.when(c == 0)
    def _():
        halo[0] = jnp.zeros((4, AUX, BS, LANES), BF16)

    @pl.when(c == COLS - 1)
    def _():
        halo[1] = jnp.zeros((4, AUX, BS, LANES), BF16)

    load_gv.wait()

    def send_b(g, d):
        return remote(
            b_send.at[g, d % 4, pl.ds((d // 4) * 16, 16)], b_in.at[g, r], b_ss.at[g, d], b_rs.at[g, r],
            {"row": d},
        )

    for g in range(2):
        @pl.when(c > 0)
        def _():
            to_right(g).wait_recv()

        @pl.when(c < COLS - 1)
        def _():
            to_left(g).wait_recv()

        @pl.loop(0, 4)
        def _(ng):
            outs = []
            for qp in range(8):
                wide = []
                for q in range(2):
                    at = g * HALF + qp * 2 + q
                    wide.append(jnp.concatenate([halo[0, ng, at], mk[ng, at], halo[1, ng, at]], axis=0))
                prod = jnp.dot(gv_ref[...], jnp.concatenate(wide, axis=1), preferred_element_type=F32)
                outs += [prod[:, :LANES], prod[:, LANES:]]
            b_send[g, ng] = jnp.transpose(jnp.stack(outs, axis=0), (1, 0, 2)).astype(BF16)

        @pl.loop(0, ROWS - 1)
        def _(i):
            send_b(g, ordered(i)).start()

        b_in[g, r] = b_send[g, ng_me, pl.ds(lg_me * 16, 16)]

    @pl.loop(1, ROWS)
    def _(k):
        s = (r + k) % ROWS
        remote(a_send.at[0, pl.ds(0, 16)], a_in.at[s], a_ss.at[s], a_rs.at[s], {"row": s}).wait_recv()

    def send_x(g, k):
        to = (x + k) % NX
        return remote(xs.at[g, k], xr.at[g, k], x_ss.at[g, k], x_rs.at[g, k], {"col": to * NY + y})

    def send_y(g, k):
        to = (y + k) % NY
        return remote(ys.at[g, to // 2], yr.at[k], y_ss.at[g, k], y_rs.at[k], {"col": x * NY + to})

    def send_z(k):
        to = (r + k) % ROWS
        return remote(zs.at[to // 4], zr.at[k], z_ss.at[k], z_rs.at[k], {"row": to})

    def chi_rows(g, ahead):
        blocks = [(x + k) % NX for k in ahead]
        for block in blocks:
            @pl.loop(4 * block, 4 * block + 4)
            def _(s):
                @pl.when(s != r)
                def _():
                    remote(
                        b_send.at[g, 0, pl.ds(0, 16)], b_in.at[g, s], b_ss.at[g, s], b_rs.at[g, s], {"row": s}
                    ).wait_recv()

        acc[...] = jnp.zeros_like(acc)

        @pl.loop(0, 8)
        def _(l):
            def pair(at, rows):
                return jnp.concatenate([at(2 * l).reshape(rows, LANES), at(2 * l + 1).reshape(rows, LANES)], axis=1)

            left = jnp.concatenate(
                [pair(lambda n: b_in[g, pl.ds(4 * block, 4), n], 4 * HALF) for block in blocks], axis=0
            )
            acc[...] += lax.dot_general(
                left, pair(lambda n: a_in[:, n], ROWS * AUX), (((1,), (1,)), ((), ())), preferred_element_type=F32
            )

    def sum_y():
        @pl.loop(1, NY)
        def _(k):
            send_y(0, k).wait_recv()

        own = part[pl.ds(pl.multiple_of((y // 2) * 16, 16), 16), :]
        for k in range(1, NY):
            own = own + yr[k].astype(F32)
        for i in range(4):
            zs[i] = own[:, i * LANES:(i + 1) * LANES]

        @pl.loop(1, ROWS)
        def _(k):
            send_z(k).start()

        zr[0] = zs[lg_me]

    for g in range(2):
        chi_rows(g, (2, 1))
        xs[g, 2] = acc[0:64, :].astype(BF16)
        send_x(g, 2).start()
        xs[g, 1] = acc[64:128, :].astype(BF16)
        send_x(g, 1).start()
        chi_rows(g, (3, 0))
        xs[g, 3] = acc[0:64, :].astype(BF16)
        send_x(g, 3).start()
        mine = acc[64:128, :]
        for k in (1, 2, 3):
            send_x(g, k).wait_recv()
            mine = mine + xr[g, k].astype(F32)

        for i in range(4):
            ys[g, i] = mine[i * 16:(i + 1) * 16, :].astype(BF16)

        @pl.loop(1, NY)
        def _(k):
            @pl.when((y + k) % 2 == g)
            def _():
                send_y(g, k).start()

        @pl.when(y % 2 == g)
        def _():
            part[...] = mine
            sum_y()

    @pl.loop(1, ROWS)
    def _(k):
        send_z(k).wait_recv()

    factor = 1.0 / math.sqrt(ORB * BS * COLS)
    tr[...] = jnp.transpose(jnp.sum(zr[...], axis=0), (1, 0))
    out_ref[...] = tr[pl.ds(pl.multiple_of(ng_me * AUX, AUX), AUX), :] * factor

    for g in range(2):
        @pl.when(c < COLS - 1)
        def _():
            to_right(g).wait_send()

        @pl.when(c > 0)
        def _():
            to_left(g).wait_send()

        for k in range(1, NX):
            send_x(g, k).wait_send()

        @pl.loop(1, NY)
        def _(k):
            @pl.when((y + k) % 2 == g)
            def _():
                send_y(g, k).wait_send()

    @pl.loop(1, ROWS)
    def _(k):
        d = (r + k) % ROWS
        send_a(d).wait_send()
        send_b(0, d).wait_send()
        send_b(1, d).wait_send()
        send_z(k).wait_send()


def on_device(tensor3, pair_mask, g_occ, g_virt_band):
    dma = pltpu.SemaphoreType.DMA
    return pl.pallas_call(
        kernel,
        out_shape=jax.ShapeDtypeStruct((AUX, 16), F32),
        in_specs=[pl.BlockSpec(memory_space=pl.ANY)] * 4,
        out_specs=pl.BlockSpec(memory_space=pltpu.VMEM),
        scratch_shapes=[
            pltpu.VMEM((AUX, BS, ORB), BF16),
            pltpu.VMEM((1, 8), jnp.int32),
            pltpu.VMEM((ORB, ORB), BF16),
            pltpu.VMEM((BS, 3 * BS), BF16),
            pltpu.VMEM((4, AUX, BS, LANES), BF16),
            pltpu.VMEM((2, 4, AUX, BS, LANES), BF16),
            pltpu.VMEM((4, BS, AUX, LANES), BF16),
            pltpu.VMEM((2, 4, BS, HALF, LANES), BF16),
            pltpu.VMEM((ROWS, PIECE, AUX, LANES), BF16),
            pltpu.VMEM((2, ROWS, PIECE, HALF, LANES), BF16),
            pltpu.VMEM((128, 512), F32),
            pltpu.VMEM((64, 512), F32),
            pltpu.VMEM((2, NX, 64, 512), BF16),
            pltpu.VMEM((2, NX, 64, 512), BF16),
            pltpu.VMEM((2, 4, 16, 512), BF16),
            pltpu.VMEM((NY, 16, 512), BF16),
            pltpu.VMEM((4, 16, LANES), F32),
            pltpu.VMEM((ROWS, 16, LANES), F32),
            pltpu.VMEM((LANES, 16), F32),
            dma((7,)), dma((2, 2)), dma((2, 2)),
            dma((ROWS,)), dma((ROWS,)), dma((2, ROWS)), dma((2, ROWS)),
            dma((2, NX)), dma((2, NX)), dma((2, NY)), dma((NY,)), dma((ROWS,)), dma((ROWS,)),
        ],
        compiler_params=pltpu.CompilerParams(
            collective_id=0, has_side_effects=True, vmem_limit_bytes=60 * 1024 * 1024
        ),
        cost_estimate=pl.CostEstimate(flops=2600000000, bytes_accessed=3 << 20, transcendentals=0),
    )(tensor3, pair_mask.T, g_occ, g_virt_band)


def solution(mesh):
    return jax.shard_map(
        on_device,
        mesh=mesh,
        in_specs=(P("row", "col", None), P(None, "col"), P(), P("col", None)),
        out_specs=P("row", "col"),
        check_vma=False,
    )
```

```python
import math

import jax
import jax.numpy as jnp
from jax import lax
from jax.experimental import pallas as pl
from jax.experimental.pallas import tpu as pltpu
from jax.sharding import PartitionSpec as P

MESH = pl.DeviceIdType.MESH
ROWS, NX, NY = 16, 4, 8
COLS = NX * NY
BS, AUX, ORB = 64, 32, 512
LANES, PIECE, HALF = 128, 16, 16
F32, BF16 = jnp.float32, jnp.bfloat16


def remote(src, dst, send, recv, where):
    return pltpu.make_async_remote_copy(
        src_ref=src, dst_ref=dst, send_sem=send, recv_sem=recv, device_id=where, device_id_type=MESH
    )


def kernel(
    m_hbm, pm_hbm, g_hbm, gv_hbm, out_ref,
    m_ref, pm_ref, g_ref, gv_ref, mk, halo, a_send, b_send, a_in, b_in,
    acc, part, xs, xr, ys, yr, zs, zr, tr,
    in_s, h_ss, h_rs, a_ss, a_rs, b_ss, b_rs, x_ss, x_rs, y_ss, y_rs, z_ss, z_rs,
):
    r = lax.axis_index("row")
    c = lax.axis_index("col")
    x, y = c // NY, c % NY
    lg_me, ng_me = r // 4, r % 4

    def load_m(i):
        return pltpu.make_async_copy(m_hbm.at[pl.ds(8 * i, 8)], m_ref.at[pl.ds(8 * i, 8)], in_s.at[i])

    load_pm = pltpu.make_async_copy(pm_hbm, pm_ref, in_s.at[4])
    load_g = pltpu.make_async_copy(g_hbm, g_ref, in_s.at[5])
    load_gv = pltpu.make_async_copy(gv_hbm, gv_ref, in_s.at[6])
    load_pm.start()
    for i in range(4):
        load_m(i).start()
    load_g.start()
    load_gv.start()

    barrier = pltpu.get_barrier_semaphore()

    def greet(where):
        pl.semaphore_signal(barrier, inc=1, device_id=where, device_id_type=MESH)

    @pl.loop(1, ROWS)
    def _(k):
        greet({"row": (r + k) % ROWS})

    for k in range(1, NX):
        greet({"col": ((x + k) % NX) * NY + y})

    @pl.loop(1, NY)
    def _(k):
        greet({"col": x * NY + (y + k) % NY})

    @pl.when(c > 0)
    def _():
        greet({"col": c - 1})

    @pl.when(c < COLS - 1)
    def _():
        greet({"col": c + 1})

    load_pm.wait()
    lane = lax.broadcasted_iota(jnp.int32, (1, ORB), 1) // BS
    keep = jnp.zeros((1, ORB), F32)
    for b in range(8):
        kept = jnp.broadcast_to((pm_ref[0:1, b:b + 1] > 0).astype(F32), (1, ORB))
        keep = jnp.where(lane == b, kept, keep)
    keep = keep.astype(BF16)

    for i in range(4):
        load_m(i).wait()

        @pl.loop(8 * i, 8 * i + 8)
        def _(p):
            row = m_ref[p] * keep
            for ng in range(4):
                mk[ng, p] = row[:, ng * LANES:(ng + 1) * LANES]

    def occ(lg):
        for ph in range(2):
            rows = [
                mk[ng, ph * 16:(ph + 1) * 16, pl.ds(pl.multiple_of(lg * 16, 16), 16), :].reshape(256, LANES)
                for ng in range(4)
            ]
            left = jnp.concatenate(rows, axis=1)
            for nh in range(2):
                part = jnp.dot(left, g_ref[:, nh * 256:(nh + 1) * 256], preferred_element_type=F32)
                for ns in range(2):
                    piece = part[:, ns * LANES:(ns + 1) * LANES].reshape(16, 16, LANES)
                    piece = jnp.transpose(piece, (1, 0, 2)).astype(BF16)
                    a_send[nh * 2 + ns, pl.ds(lg * 16, 16), ph * 16:(ph + 1) * 16, :] = piece

    def send_a(d):
        return remote(
            a_send.at[d % 4, pl.ds((d // 4) * 16, 16)], a_in.at[r], a_ss.at[d], a_rs.at[r], {"row": d}
        )

    load_g.wait()

    @pl.loop(0, 4)
    def _(lg):
        occ(lg)

    both = (c > 0).astype(jnp.int32) + (c < COLS - 1).astype(jnp.int32)
    pl.semaphore_wait(barrier, ROWS - 1 + NX - 1 + NY - 1 + both)

    def half_of(ref, g):
        return ref.at[:, pl.ds(HALF * g, HALF)]

    def to_right(g):
        return remote(half_of(mk, g), half_of(halo.at[0], g), h_ss.at[0, g], h_rs.at[0, g], {"col": c + 1})

    def to_left(g):
        return remote(half_of(mk, g), half_of(halo.at[1], g), h_ss.at[1, g], h_rs.at[1, g], {"col": c - 1})

    def steps(i, count):
        near = (count - 1 - i) // 2 + 1
        return near + ((count - 1 - i) % 2) * (count + 1 - 2 * near)

    def ordered(i):
        return (r + steps(i, ROWS - 1)) % ROWS

    @pl.loop(0, 4)
    def _(i):
        send_a(ordered(i)).start()

    for g in range(2):
        @pl.when(c < COLS - 1)
        def _():
            to_right(g).start()

        @pl.when(c > 0)
        def _():
            to_left(g).start()

    @pl.loop(4, ROWS - 1)
    def _(i):
        send_a(ordered(i)).start()

    a_in[r] = a_send[ng_me, pl.ds(lg_me * 16, 16)]

    @pl.when(c == 0)
    def _():
        halo[0] = jnp.zeros((4, AUX, BS, LANES), BF16)

    @pl.when(c == COLS - 1)
    def _():
        halo[1] = jnp.zeros((4, AUX, BS, LANES), BF16)

    load_gv.wait()

    def send_b(g, d):
        return remote(
            b_send.at[g, d % 4, pl.ds((d // 4) * 16, 16)], b_in.at[g, r], b_ss.at[g, d], b_rs.at[g, r],
            {"row": d},
        )

    for g in range(2):
        @pl.when(c > 0)
        def _():
            to_right(g).wait_recv()

        @pl.when(c < COLS - 1)
        def _():
            to_left(g).wait_recv()

        @pl.loop(0, 4)
        def _(ng):
            outs = []
            for qp in range(8):
                wide = []
                for q in range(2):
                    at = g * HALF + qp * 2 + q
                    wide.append(jnp.concatenate([halo[0, ng, at], mk[ng, at], halo[1, ng, at]], axis=0))
                prod = jnp.dot(gv_ref[...], jnp.concatenate(wide, axis=1), preferred_element_type=F32)
                outs += [prod[:, :LANES], prod[:, LANES:]]
            b_send[g, ng] = jnp.transpose(jnp.stack(outs, axis=0), (1, 0, 2)).astype(BF16)

        @pl.loop(0, ROWS - 1)
        def _(i):
            send_b(g, ordered(i)).start()

        b_in[g, r] = b_send[g, ng_me, pl.ds(lg_me * 16, 16)]

    @pl.loop(1, ROWS)
    def _(k):
        s = (r + k) % ROWS
        remote(a_send.at[0, pl.ds(0, 16)], a_in.at[s], a_ss.at[s], a_rs.at[s], {"row": s}).wait_recv()

    def send_x(g, k):
        to = (x + k) % NX
        return remote(xs.at[g, k], xr.at[g, k], x_ss.at[g, k], x_rs.at[g, k], {"col": to * NY + y})

    def send_y(g, k):
        to = (y + k) % NY
        return remote(ys.at[g, to // 2], yr.at[k], y_ss.at[g, k], y_rs.at[k], {"col": x * NY + to})

    def send_z(k):
        to = (r + k) % ROWS
        return remote(zs.at[to // 4, to % 2], zr.at[k], z_ss.at[k], z_rs.at[k], {"row": to})

    def chi_rows(g, ahead):
        blocks = [(x + k) % NX for k in ahead]
        for block in blocks:
            @pl.loop(4 * block, 4 * block + 4)
            def _(s):
                @pl.when(s != r)
                def _():
                    remote(
                        b_send.at[g, 0, pl.ds(0, 16)], b_in.at[g, s], b_ss.at[g, s], b_rs.at[g, s], {"row": s}
                    ).wait_recv()

        def wide(at, rows):
            return jnp.concatenate([at(n).reshape(rows, LANES) for n in range(PIECE)], axis=1)

        left = jnp.concatenate(
            [wide(lambda n: b_in[g, pl.ds(4 * block, 4), n], 4 * HALF) for block in blocks], axis=0
        )
        for p in range(2):
            acc[:, 256 * p:256 * p + 256] = lax.dot_general(
                left, wide(lambda n: a_in[8 * p:8 * p + 8, n], 256), (((1,), (1,)), ((), ())), preferred_element_type=F32
            )

    def sum_y():
        @pl.loop(1, NY)
        def _(k):
            send_y(0, k).wait_recv()

        own = part[pl.ds(pl.multiple_of((y // 2) * 16, 16), 16), :]
        for k in range(1, NY):
            own = own + yr[k].astype(F32)
        lanes = lax.broadcasted_iota(jnp.int32, (8, LANES), 1) // AUX
        for i in range(4):
            upper, lower = own[:8, i * LANES:(i + 1) * LANES], own[8:, i * LANES:(i + 1) * LANES]
            zs[i, 0] = jnp.where(lanes % 2 == 0, upper, pltpu.roll(lower, AUX, 1))
            zs[i, 1] = jnp.where(lanes % 2 == 1, upper, pltpu.roll(lower, AUX, 1))

        @pl.loop(0, ROWS - 1)
        def _(i):
            send_z(steps(i, ROWS - 1)).start()

        zr[0] = zs[lg_me, ng_me % 2]

    for g in range(2):
        chi_rows(g, (2, 1))
        xs[g, 2] = acc[0:64, :].astype(BF16)
        send_x(g, 2).start()
        xs[g, 1] = acc[64:128, :].astype(BF16)
        send_x(g, 1).start()
        chi_rows(g, (3, 0))
        xs[g, 3] = acc[0:64, :].astype(BF16)
        send_x(g, 3).start()
        mine = acc[64:128, :]
        for k in (1, 2, 3):
            send_x(g, k).wait_recv()
            mine = mine + xr[g, k].astype(F32)

        for i in range(4):
            ys[g, i] = mine[i * 16:(i + 1) * 16, :].astype(BF16)

        @pl.loop(0, NY - 1)
        def _(i):
            k = steps(i, NY - 1)

            @pl.when((y + k) % 2 == g)
            def _():
                send_y(g, k).start()

        @pl.when(y % 2 == g)
        def _():
            part[...] = mine
            sum_y()

    @pl.loop(1, ROWS)
    def _(k):
        send_z(k).wait_recv()

    factor = 1.0 / math.sqrt(ORB * BS * COLS)
    tr[...] = jnp.transpose(jnp.sum(zr[...], axis=0), (1, 0))
    upper = tr[pl.ds(pl.multiple_of(ng_me * AUX, AUX), AUX), :]
    lower = tr[pl.ds(pl.multiple_of((ng_me + 1) % 4 * AUX, AUX), AUX), :]
    out_ref[...] = jnp.concatenate([upper, lower], axis=1) * factor

    for g in range(2):
        @pl.when(c < COLS - 1)
        def _():
            to_right(g).wait_send()

        @pl.when(c > 0)
        def _():
            to_left(g).wait_send()

        for k in range(1, NX):
            send_x(g, k).wait_send()

        @pl.loop(1, NY)
        def _(k):
            @pl.when((y + k) % 2 == g)
            def _():
                send_y(g, k).wait_send()

    @pl.loop(1, ROWS)
    def _(k):
        d = (r + k) % ROWS
        send_a(d).wait_send()
        send_b(0, d).wait_send()
        send_b(1, d).wait_send()
        send_z(k).wait_send()


def on_device(tensor3, pair_mask, g_occ, g_virt_band):
    dma = pltpu.SemaphoreType.DMA
    return pl.pallas_call(
        kernel,
        out_shape=jax.ShapeDtypeStruct((AUX, 16), F32),
        in_specs=[pl.BlockSpec(memory_space=pl.ANY)] * 4,
        out_specs=pl.BlockSpec(memory_space=pltpu.VMEM),
        scratch_shapes=[
            pltpu.VMEM((AUX, BS, ORB), BF16),
            pltpu.VMEM((1, 8), jnp.int32),
            pltpu.VMEM((ORB, ORB), BF16),
            pltpu.VMEM((BS, 3 * BS), BF16),
            pltpu.VMEM((4, AUX, BS, LANES), BF16),
            pltpu.VMEM((2, 4, AUX, BS, LANES), BF16),
            pltpu.VMEM((4, BS, AUX, LANES), BF16),
            pltpu.VMEM((2, 4, BS, HALF, LANES), BF16),
            pltpu.VMEM((ROWS, PIECE, AUX, LANES), BF16),
            pltpu.VMEM((2, ROWS, PIECE, HALF, LANES), BF16),
            pltpu.VMEM((128, 512), F32),
            pltpu.VMEM((64, 512), F32),
            pltpu.VMEM((2, NX, 64, 512), BF16),
            pltpu.VMEM((2, NX, 64, 512), BF16),
            pltpu.VMEM((2, 4, 16, 512), BF16),
            pltpu.VMEM((NY, 16, 512), BF16),
            pltpu.VMEM((4, 2, 8, LANES), F32),
            pltpu.VMEM((ROWS, 8, LANES), F32),
            pltpu.VMEM((LANES, 8), F32),
            dma((7,)), dma((2, 2)), dma((2, 2)),
            dma((ROWS,)), dma((ROWS,)), dma((2, ROWS)), dma((2, ROWS)),
            dma((2, NX)), dma((2, NX)), dma((2, NY)), dma((NY,)), dma((ROWS,)), dma((ROWS,)),
        ],
        compiler_params=pltpu.CompilerParams(
            collective_id=0, has_side_effects=True, vmem_limit_bytes=60 * 1024 * 1024
        ),
        cost_estimate=pl.CostEstimate(flops=2600000000, bytes_accessed=3 << 20, transcendentals=0),
    )(tensor3, pair_mask.T, g_occ, g_virt_band)


def solution(mesh):
    return jax.shard_map(
        on_device,
        mesh=mesh,
        in_specs=(P("row", "col", None), P(None, "col"), P(), P("col", None)),
        out_specs=P("row", "col"),
        check_vma=False,
    )
```

```python
import math

import jax
import jax.numpy as jnp
from jax import lax
from jax.experimental import pallas as pl
from jax.experimental.pallas import tpu as pltpu
from jax.sharding import PartitionSpec as P

MESH = pl.DeviceIdType.MESH
ROWS, NX, NY = 16, 4, 8
COLS = NX * NY
BS, AUX, ORB = 64, 32, 512
LANES, PIECE, HALF = 128, 16, 16
F32, BF16 = jnp.float32, jnp.bfloat16


def remote(src, dst, send, recv, where):
    return pltpu.make_async_remote_copy(
        src_ref=src, dst_ref=dst, send_sem=send, recv_sem=recv, device_id=where, device_id_type=MESH
    )


def kernel(
    m_hbm, pm_hbm, g_hbm, gv_hbm, out_ref,
    m_ref, pm_ref, g_ref, gv_ref, mk, halo, a_send, b_send, a_in, b_in,
    acc, full, part, xs, xr, ys, yr, zs, zr, tr,
    in_s, h_ss, h_rs, a_ss, a_rs, b_ss, b_rs, x_ss, x_rs, y_ss, y_rs, z_ss, z_rs,
):
    r = lax.axis_index("row")
    c = lax.axis_index("col")
    x, y = c // NY, c % NY
    lg_me, ng_me = r // 4, r % 4

    def load_m(i):
        return pltpu.make_async_copy(m_hbm.at[pl.ds(8 * i, 8)], m_ref.at[pl.ds(8 * i, 8)], in_s.at[i])

    load_pm = pltpu.make_async_copy(pm_hbm, pm_ref, in_s.at[4])
    load_g = pltpu.make_async_copy(g_hbm, g_ref, in_s.at[5])
    load_gv = pltpu.make_async_copy(gv_hbm, gv_ref, in_s.at[6])
    def steps(i, count):
        near = (count - 1 - i) // 2 + 1
        return near + ((count - 1 - i) % 2) * (count + 1 - 2 * near)

    barrier = pltpu.get_barrier_semaphore()

    def greet(where):
        pl.semaphore_signal(barrier, inc=1, device_id=where, device_id_type=MESH)

    for i in range(4):
        greet({"row": (r + steps(i, ROWS - 1)) % ROWS})
        greet({"col": x * NY + (y + steps(i, NY - 1)) % NY})

    @pl.loop(4, ROWS - 1)
    def _(i):
        greet({"row": (r + steps(i, ROWS - 1)) % ROWS})

    for i in range(4, NY - 1):
        greet({"col": x * NY + (y + steps(i, NY - 1)) % NY})

    for k in range(1, NX):
        greet({"col": ((x + k) % NX) * NY + y})

    @pl.when(c > 0)
    def _():
        greet({"col": c - 1})

    @pl.when(c < COLS - 1)
    def _():
        greet({"col": c + 1})

    load_pm.start()
    for i in range(4):
        load_m(i).start()
    load_g.start()
    load_gv.start()

    load_pm.wait()
    lane = lax.broadcasted_iota(jnp.int32, (1, ORB), 1) // BS
    keep = jnp.zeros((1, ORB), F32)
    for b in range(8):
        kept = jnp.broadcast_to((pm_ref[0:1, b:b + 1] > 0).astype(F32), (1, ORB))
        keep = jnp.where(lane == b, kept, keep)
    keep = keep.astype(BF16)

    for i in range(4):
        load_m(i).wait()

        @pl.loop(8 * i, 8 * i + 8)
        def _(p):
            row = m_ref[p] * keep
            for ng in range(4):
                mk[ng, p] = row[:, ng * LANES:(ng + 1) * LANES]

    def occ(lg):
        for ph in range(2):
            rows = [
                mk[ng, ph * 16:(ph + 1) * 16, pl.ds(pl.multiple_of(lg * 16, 16), 16), :].reshape(256, LANES)
                for ng in range(4)
            ]
            left = jnp.concatenate(rows, axis=1)
            for nh in range(2):
                part = jnp.dot(left, g_ref[:, nh * 256:(nh + 1) * 256], preferred_element_type=F32)
                for ns in range(2):
                    piece = part[:, ns * LANES:(ns + 1) * LANES].reshape(16, 16, LANES)
                    piece = jnp.transpose(piece, (1, 0, 2)).astype(BF16)
                    a_send[nh * 2 + ns, pl.ds(lg * 16, 16), ph * 16:(ph + 1) * 16, :] = piece

    def send_a(d):
        return remote(
            a_send.at[d % 4, pl.ds((d // 4) * 16, 16)], a_in.at[r], a_ss.at[d], a_rs.at[r], {"row": d}
        )

    load_g.wait()

    @pl.loop(0, 4)
    def _(lg):
        occ(lg)

    both = (c > 0).astype(jnp.int32) + (c < COLS - 1).astype(jnp.int32)
    pl.semaphore_wait(barrier, ROWS - 1 + NX - 1 + NY - 1 + both)

    def half_of(ref, g):
        return ref.at[:, pl.ds(HALF * g, HALF)]

    def to_right(g):
        return remote(half_of(mk, g), half_of(halo.at[0], g), h_ss.at[0, g], h_rs.at[0, g], {"col": c + 1})

    def to_left(g):
        return remote(half_of(mk, g), half_of(halo.at[1], g), h_ss.at[1, g], h_rs.at[1, g], {"col": c - 1})

    def ordered(i):
        return (r + steps(i, ROWS - 1)) % ROWS

    @pl.loop(0, 4)
    def _(i):
        send_a(ordered(i)).start()

    for g in range(2):
        @pl.when(c < COLS - 1)
        def _():
            to_right(g).start()

        @pl.when(c > 0)
        def _():
            to_left(g).start()

    @pl.loop(4, ROWS - 1)
    def _(i):
        send_a(ordered(i)).start()

    a_in[r] = a_send[ng_me, pl.ds(lg_me * 16, 16)]

    @pl.when(c == 0)
    def _():
        halo[0] = jnp.zeros((4, AUX, BS, LANES), BF16)

    @pl.when(c == COLS - 1)
    def _():
        halo[1] = jnp.zeros((4, AUX, BS, LANES), BF16)

    load_gv.wait()

    def send_b(g, d):
        return remote(
            b_send.at[g, d % 4, pl.ds((d // 4) * 16, 16)], b_in.at[g, r], b_ss.at[g, d], b_rs.at[g, r],
            {"row": d},
        )

    for g in range(2):
        @pl.when(c > 0)
        def _():
            to_right(g).wait_recv()

        @pl.when(c < COLS - 1)
        def _():
            to_left(g).wait_recv()

        @pl.loop(0, 4)
        def _(ng):
            outs = []
            for qp in range(8):
                wide = []
                for q in range(2):
                    at = g * HALF + qp * 2 + q
                    wide.append(jnp.concatenate([halo[0, ng, at], mk[ng, at], halo[1, ng, at]], axis=0))
                prod = jnp.dot(gv_ref[...], jnp.concatenate(wide, axis=1), preferred_element_type=F32)
                outs += [prod[:, :LANES], prod[:, LANES:]]
            b_send[g, ng] = jnp.transpose(jnp.stack(outs, axis=0), (1, 0, 2)).astype(BF16)

        @pl.loop(0, ROWS - 1)
        def _(i):
            send_b(g, ordered(i)).start()

        b_in[g, r] = b_send[g, ng_me, pl.ds(lg_me * 16, 16)]

    @pl.loop(1, ROWS)
    def _(k):
        s = (r + k) % ROWS
        remote(a_send.at[0, pl.ds(0, 16)], a_in.at[s], a_ss.at[s], a_rs.at[s], {"row": s}).wait_recv()

    def send_x(g, k):
        to = (x + k) % NX
        return remote(xs.at[g, k], xr.at[g, k], x_ss.at[g, k], x_rs.at[g, k], {"col": to * NY + y})

    def send_y(g, k):
        to = (y + k) % NY
        return remote(ys.at[g, to // 2], yr.at[k], y_ss.at[g, k], y_rs.at[k], {"col": x * NY + to})

    def send_z(k):
        to = (r + k) % ROWS
        return remote(zs.at[to // 4, to % 2], zr.at[k], z_ss.at[k], z_rs.at[k], {"row": to})

    def chi_rows(g, ahead):
        blocks = [(lg_me + k) % NX for k in ahead]
        for block in blocks:
            @pl.loop(4 * block, 4 * block + 4)
            def _(s):
                @pl.when(s != r)
                def _():
                    remote(
                        b_send.at[g, 0, pl.ds(0, 16)], b_in.at[g, s], b_ss.at[g, s], b_rs.at[g, s], {"row": s}
                    ).wait_recv()

        def wide(at, rows):
            return jnp.concatenate([at(n).reshape(rows, LANES) for n in range(PIECE)], axis=1)

        left = jnp.concatenate(
            [wide(lambda n: b_in[g, pl.ds(4 * block, 4), n], 4 * HALF) for block in blocks], axis=0
        )
        for p in range(2):
            acc[0:64 * len(ahead), 256 * p:256 * p + 256] = lax.dot_general(
                left, wide(lambda n: a_in[8 * p:8 * p + 8, n], 256), (((1,), (1,)), ((), ())), preferred_element_type=F32
            )

    def sum_y():
        @pl.loop(1, NY)
        def _(k):
            send_y(0, k).wait_recv()

        own = part[pl.ds(pl.multiple_of((y // 2) * 16, 16), 16), :]
        for k in range(1, NY):
            own = own + yr[k].astype(F32)
        lanes = lax.broadcasted_iota(jnp.int32, (8, LANES), 1) // AUX
        for i in range(4):
            upper, lower = own[:8, i * LANES:(i + 1) * LANES], own[8:, i * LANES:(i + 1) * LANES]
            zs[i, 0] = jnp.where(lanes % 2 == 0, upper, pltpu.roll(lower, AUX, 1))
            zs[i, 1] = jnp.where(lanes % 2 == 1, upper, pltpu.roll(lower, AUX, 1))

        @pl.loop(0, ROWS - 1)
        def _(i):
            send_z(steps(i, ROWS - 1)).start()

        zr[0] = zs[lg_me, ng_me % 2]

    def left_xy(g):
        for k in range(1, NX):
            send_x(g, k).wait_send()

        @pl.loop(1, NY)
        def _(k):
            @pl.when((y + k) % 2 == g)
            def _():
                send_y(g, k).wait_send()

    def left_row(send):
        @pl.loop(1, ROWS)
        def _(k):
            send((r + k) % ROWS).wait_send()

    for g in range(2):
        if g == 1:
            for h in range(2):
                @pl.when(c < COLS - 1)
                def _():
                    to_right(h).wait_send()

                @pl.when(c > 0)
                def _():
                    to_left(h).wait_send()

            left_row(send_a)
            left_row(lambda d: send_b(0, d))
            left_xy(0)

        for ahead in ((2,), (1, 3), (0,)):
            chi_rows(g, ahead)
            for at, k in enumerate(ahead):
                rows = acc[64 * at:64 * at + 64, :]
                step = (lg_me + k - x + NX) % NX

                @pl.when(step == 0)
                def _():
                    full[...] = rows

                @pl.when(step != 0)
                def _():
                    xs[g, step] = rows.astype(BF16)
                    send_x(g, step).start()

        if g == 1:
            left_row(lambda d: send_b(1, d))
        mine = full[...]
        for k in (1, 2, 3):
            send_x(g, k).wait_recv()
            mine = mine + xr[g, k].astype(F32)

        for i in range(4):
            ys[g, i] = mine[i * 16:(i + 1) * 16, :].astype(BF16)

        @pl.loop(0, NY - 1)
        def _(i):
            k = steps(i, NY - 1)

            @pl.when((y + k) % 2 == g)
            def _():
                send_y(g, k).start()

        @pl.when(y % 2 == g)
        def _():
            part[...] = mine
            sum_y()

    left_xy(1)

    @pl.loop(1, ROWS)
    def _(k):
        send_z(k).wait_recv()

    factor = 1.0 / math.sqrt(ORB * BS * COLS)
    tr[...] = jnp.transpose(jnp.sum(zr[...], axis=0), (1, 0))
    upper = tr[pl.ds(pl.multiple_of(ng_me * AUX, AUX), AUX), :]
    lower = tr[pl.ds(pl.multiple_of((ng_me + 1) % 4 * AUX, AUX), AUX), :]
    out_ref[...] = jnp.concatenate([upper, lower], axis=1) * factor

    @pl.loop(1, ROWS)
    def _(k):
        send_z(k).wait_send()


def on_device(tensor3, pair_mask, g_occ, g_virt_band):
    dma = pltpu.SemaphoreType.DMA
    return pl.pallas_call(
        kernel,
        out_shape=jax.ShapeDtypeStruct((AUX, 16), F32),
        in_specs=[pl.BlockSpec(memory_space=pl.ANY)] * 4,
        out_specs=pl.BlockSpec(memory_space=pltpu.VMEM),
        scratch_shapes=[
            pltpu.VMEM((AUX, BS, ORB), BF16),
            pltpu.VMEM((1, 8), jnp.int32),
            pltpu.VMEM((ORB, ORB), BF16),
            pltpu.VMEM((BS, 3 * BS), BF16),
            pltpu.VMEM((4, AUX, BS, LANES), BF16),
            pltpu.VMEM((2, 4, AUX, BS, LANES), BF16),
            pltpu.VMEM((4, BS, AUX, LANES), BF16),
            pltpu.VMEM((2, 4, BS, HALF, LANES), BF16),
            pltpu.VMEM((ROWS, PIECE, AUX, LANES), BF16),
            pltpu.VMEM((2, ROWS, PIECE, HALF, LANES), BF16),
            pltpu.VMEM((128, 512), F32),
            pltpu.VMEM((64, 512), F32),
            pltpu.VMEM((64, 512), F32),
            pltpu.VMEM((2, NX, 64, 512), BF16),
            pltpu.VMEM((2, NX, 64, 512), BF16),
            pltpu.VMEM((2, 4, 16, 512), BF16),
            pltpu.VMEM((NY, 16, 512), BF16),
            pltpu.VMEM((4, 2, 8, LANES), F32),
            pltpu.VMEM((ROWS, 8, LANES), F32),
            pltpu.VMEM((LANES, 8), F32),
            dma((7,)), dma((2, 2)), dma((2, 2)),
            dma((ROWS,)), dma((ROWS,)), dma((2, ROWS)), dma((2, ROWS)),
            dma((2, NX)), dma((2, NX)), dma((2, NY)), dma((NY,)), dma((ROWS,)), dma((ROWS,)),
        ],
        compiler_params=pltpu.CompilerParams(
            collective_id=0, has_side_effects=True, vmem_limit_bytes=60 * 1024 * 1024
        ),
        cost_estimate=pl.CostEstimate(flops=2600000000, bytes_accessed=3 << 20, transcendentals=0),
    )(tensor3, pair_mask.T, g_occ, g_virt_band)


def solution(mesh):
    return jax.shard_map(
        on_device,
        mesh=mesh,
        in_specs=(P("row", "col", None), P(None, "col"), P(), P("col", None)),
        out_specs=P("row", "col"),
        check_vma=False,
    )
```
